256 devices in a mesh: rx: 8 (over y_lo, x), ry: 8 (over z), tp: 4 (over y_hi, core).
Axes of the slice: x: 4, y: 4 (y_hi: 2, y_lo: 2; y = y_hi * 2 + y_lo), z: 8, core: 2. Of those that a mesh axis runs over, the one named last changes fastest.
Arguments:
- inputs: bfloat16 [8, 8, 512, 6144], P('rx', 'ry', None, 'tp'), may hold values from -6 to 6
- out_grads: bfloat16 [8, 8, 512, 6144], P('rx', 'ry', None, 'tp'), may hold values from -6 to 6
- up_weight: bfloat16 [8, 8, 256, 6144], P('rx', 'ry', 'tp'), may hold values from -6 to 6
- down_weight: bfloat16 [8, 8, 256, 6144], P('rx', 'ry', 'tp'), may hold values from -6 to 6
- group_x: int32 [8, 8], replicated, may hold values from 0 to 1
- group_y: int32 [8, 8], replicated, may hold values from 0 to 1
Outputs:
- input_grads: bfloat16 [8, 8, 512, 6144], P('rx', 'ry', None, 'tp')
- new_up: bfloat16 [8, 8, 256, 6144], P('rx', 'ry', 'tp')
- new_down: bfloat16 [8, 8, 256, 6144], P('rx', 'ry', 'tp')
The draws below stay inside these ranges and needn't reach their ends.
Inputs may be any that keep to these rules, and one draw needn't show every extreme that they name: `group_x`: group labels; replicas of one line with equal labels form one group. `group_y`: group labels; replicas of one line with equal labels form one group.
All inputs are finite; a program needn't handle non-finite values.
Results may differ from the reference program's by a relative error of at most 0.02.
Values may be sent and summed in bfloat16 or wider, within the bound.
No kernel may reach another device: no remote copies, remote signals or barrier semaphores. Data moves between devices by JAX's collectives and lax.ppermute only.
A program may use at most 128 MiB of HBM per device.

```python
import jax
import jax.numpy as jnp
from jax import lax

D = 6144
TOK = 512
GROUPS = 2
HID = 256
N_RX = 8
N_RY = 8


def set_ends(drawn, key, low, high):
    dims = drawn.shape
    place = [jax.random.randint(jax.random.fold_in(key, axis), (), 0, dims[axis]) for axis in range(len(dims))]
    drawn = drawn.at[tuple(place)].set(low)
    longest = dims.index(max(dims))
    place[longest] = (place[longest] + 1) % dims[longest]
    return drawn.at[tuple(place)].set(high)


def steps_of(key, shape, split, smallest, largest):
    def one(dim, blocks):
        steps = jax.random.uniform(jax.random.fold_in(jax.random.fold_in(key, 6), dim), (blocks,), jnp.float32, smallest / len(split), largest / len(split))
        return jnp.repeat(jnp.exp(steps), shape[dim] // blocks).reshape((-1,) + (1,) * (len(shape) - dim - 1))

    gain = one(*split[0])
    for cut in split[1:]:
        gain = gain * one(*cut)
    return gain


def noise(key, extent, deviation, reach, split=(), kind=jnp.bfloat16):
    entries = jax.random.normal(key, extent, jnp.float32) * deviation
    if len(split) > 0:
        entries = steps_of(key, extent, split, -0.22, 0.18) * entries
    return jnp.clip(entries, min=-reach, max=reach).astype(kind)


def setup_inputs(seed: int = 0) -> dict:
    keys = jax.random.split(jax.random.key(seed), 7)
    inputs = noise(keys[0], (N_RX, N_RY, TOK, D), 1.0, 6.0, ((0, 8), (1, 8), (3, 4)))
    out_grads = noise(keys[1], (N_RX, N_RY, TOK, D), 1.0, 6.0, ((0, 8), (1, 8), (3, 4)))
    up_weight = noise(keys[2], (N_RX, N_RY, HID, D), 1.0, 6.0, ((0, 8), (1, 8), (2, 4)))
    down_weight = noise(keys[3], (N_RX, N_RY, HID, D), 1.0, 6.0, ((0, 8), (1, 8), (2, 4)))
    group_x = set_ends(jax.random.randint(keys[4], (N_RY, N_RX), 0, GROUPS), jax.random.fold_in(keys[4], 1), 0, GROUPS - 1).astype(jnp.int32)
    group_y = set_ends(jax.random.randint(keys[5], (N_RX, N_RY), 0, GROUPS), jax.random.fold_in(keys[5], 1), 0, GROUPS - 1).astype(jnp.int32)
    return {"inputs": inputs, "out_grads": out_grads, "up_weight": up_weight, "down_weight": down_weight, "group_x": group_x, "group_y": group_y}


learn_rate = 0.5
inv_root_two = 0.7071067811865476
inv_root_tau = 0.3989422804014327


def replica_step(x, dy, up_w, down_w):
    scale_in = D ** -0.5
    scale_hid = HID ** -0.5
    pre = jnp.dot(x, up_w.T, preferred_element_type=jnp.float32) * scale_in
    hid_grad = jnp.dot(dy, down_w.T, preferred_element_type=jnp.float32) * scale_hid
    cdf = 0.5 * (1.0 + jax.scipy.special.erf(pre * inv_root_two))
    act = (pre * cdf).astype(jnp.bfloat16)
    pre_grad = (hid_grad * (cdf + pre * jnp.exp(-0.5 * pre * pre) * inv_root_tau)).astype(jnp.bfloat16)
    in_grad = (jnp.dot(pre_grad, up_w, preferred_element_type=jnp.float32) * scale_in).astype(jnp.bfloat16)
    grad_up = jnp.dot(pre_grad.T, x, preferred_element_type=jnp.float32) * scale_in
    grad_down = jnp.dot(act.T, dy, preferred_element_type=jnp.float32) * scale_hid
    step_up = (up_w.astype(jnp.float32) - learn_rate * grad_up).astype(jnp.bfloat16)
    step_down = (down_w.astype(jnp.float32) - learn_rate * grad_down).astype(jnp.bfloat16)
    return in_grad, step_up, step_down


def reference(inputs, out_grads, up_weight, down_weight, group_x, group_y):
    count = N_RX * N_RY
    flat = lambda arr: arr.reshape((count,) + arr.shape[2:])
    in_grad, step_up, step_down = lax.map(lambda item: replica_step(*item), (flat(inputs), flat(out_grads), flat(up_weight), flat(down_weight)))
    unflat = lambda arr: arr.reshape((N_RX, N_RY) + arr.shape[1:])
    in_grad, step_up, step_down = unflat(in_grad), unflat(step_up), unflat(step_down)
    mask_first = (group_x[:, :, None] == group_x[:, None, :]).astype(jnp.float32)
    count_first = jnp.sum(mask_first, axis=2).T
    mask_second = (group_y[:, :, None] == group_y[:, None, :]).astype(jnp.float32)
    count_second = jnp.sum(mask_second, axis=2)

    def first_round(weights):
        sums = jnp.einsum('jik,kjhd->ijhd', mask_first, weights.astype(jnp.float32), precision=lax.Precision.HIGHEST)
        return (sums / count_first[:, :, None, None]).astype(jnp.bfloat16)

    def second_round(weights):
        sums = jnp.einsum('ijk,ikhd->ijhd', mask_second, weights.astype(jnp.float32), precision=lax.Precision.HIGHEST)
        return (sums / count_second[:, :, None, None]).astype(jnp.bfloat16)

    new_up = second_round(first_round(step_up))
    new_down = second_round(first_round(step_down))
    return in_grad, new_up, new_down
```

```python
import jax
import jax.numpy as jnp
from jax import lax
from jax.sharding import PartitionSpec as P

GROUPS = 2

learn_rate = 0.5
inv_root_two = 0.7071067811865476
inv_root_tau = 0.3989422804014327


def dot(left, right, dims):
    return lax.dot_general(left, right, (dims, ((), ())), preferred_element_type=jnp.float32)


def group_means(terms, labels):
    terms = terms.astype(jnp.float32)
    means = []
    for slot in range(GROUPS):
        member = (labels == slot).astype(jnp.float32)
        total = sum(terms[k] * member[k] for k in range(terms.shape[0]))
        means.append((total / jnp.maximum(jnp.sum(member), 1.0)).astype(jnp.bfloat16))
    return jnp.stack(means)


def shards(inputs, out_grads, up_weight, down_weight, group_x, group_y):
    x = inputs[0, 0]
    dy = out_grads[0, 0]
    tok, feat = x.shape
    rows, width = up_weight.shape[2:]
    n_tp = lax.axis_size("tp")
    n_rx = lax.axis_size("rx")
    n_ry = lax.axis_size("ry")
    hid = rows * n_tp
    scale_in = width ** (-0.5)
    scale_hid = hid ** (-0.5)
    first_pos = lax.axis_index("rx")
    second_pos = lax.axis_index("ry")

    both = jnp.stack([up_weight[0, 0], down_weight[0, 0]])
    both = both.reshape(2, rows, n_tp, feat).transpose(2, 0, 1, 3)
    both = lax.all_to_all(both, "tp", 0, 0)
    up = both[:, 0].reshape(hid, feat)
    down = both[:, 1].reshape(hid, feat)

    pre_part = dot(x, up, ((1,), (1,))).astype(jnp.bfloat16)
    hid_part = dot(dy, down, ((1,), (1,))).astype(jnp.bfloat16)
    parts = jnp.stack([pre_part, hid_part]).reshape(2, n_tp, tok // n_tp, hid).transpose(1, 0, 2, 3)
    parts = lax.all_to_all(parts, "tp", 0, 0)
    sums = jnp.sum(parts.astype(jnp.float32), axis=0)
    pre = sums[0] * scale_in
    hid_grad = sums[1] * scale_hid
    cdf = 0.5 * (1.0 + lax.erf(pre * inv_root_two))
    act = (pre * cdf).astype(jnp.bfloat16)
    pre_grad = (hid_grad * (cdf + pre * jnp.exp(-0.5 * pre * pre) * inv_root_tau)).astype(jnp.bfloat16)
    own = jnp.stack([act, pre_grad])
    whole = lax.all_to_all(jnp.broadcast_to(own[None], (n_tp,) + own.shape), "tp", 0, 0)
    act = whole[:, 0].reshape(tok, hid)
    pre_grad = whole[:, 1].reshape(tok, hid)

    in_grad = (dot(pre_grad, up, ((1,), (0,))) * scale_in).astype(jnp.bfloat16)
    grad_up = dot(pre_grad, x, ((0,), (0,))) * scale_in
    grad_down = dot(act, dy, ((0,), (0,))) * scale_hid
    step_up = (up.astype(jnp.float32) - learn_rate * grad_up).astype(jnp.bfloat16)
    step_down = (down.astype(jnp.float32) - learn_rate * grad_down).astype(jnp.bfloat16)

    slab = rows // n_rx
    quarter = feat // (n_ry // 2)
    steps = jnp.stack([step_up, step_down]).reshape(2, n_tp, n_rx, slab, feat)
    steps = lax.all_to_all(steps.transpose(2, 0, 1, 3, 4), "rx", 0, 0)
    mids = group_means(steps, group_x[second_pos])

    mids = mids.reshape(GROUPS, 2, n_tp, slab, n_ry // 2, quarter).transpose(1, 4, 2, 0, 3, 5)
    mids = mids.reshape(n_ry * n_tp, GROUPS, slab, quarter)
    mids = lax.all_to_all(mids, ("ry", "tp"), 0, 0)
    mids = mids.reshape(n_ry, n_tp, GROUPS, slab, quarter)
    news = []
    for i in range(n_rx):
        chosen = group_x[:, i][:, None, None, None] == 0
        news.append(group_means(jnp.where(chosen, mids[:, :, 0], mids[:, :, 1]), group_y[i]))
    news = jnp.stack(news)
    news = lax.all_to_all(news, "rx", 0, 0)
    labels = group_y[first_pos]
    news = jnp.where(labels[:, None, None, None, None] == 0, news[None, :, 0], news[None, :, 1])
    news = lax.all_to_all(news, "ry", 0, 0)
    news = news.reshape(2, n_ry // 2, n_rx, n_tp, slab, quarter).transpose(0, 2, 4, 3, 1, 5)
    news = news.reshape(2, rows, width)
    return (in_grad[None, None], news[0][None, None], news[1][None, None])


def solution(mesh):
    in_specs = (
        P("rx", "ry", None, "tp"),
        P("rx", "ry", None, "tp"),
        P("rx", "ry", "tp", None),
        P("rx", "ry", "tp", None),
        P(),
        P(),
    )
    out_specs = (P("rx", "ry", None, "tp"), P("rx", "ry", "tp", None), P("rx", "ry", "tp", None))
    return jax.shard_map(shards, mesh=mesh, in_specs=in_specs, out_specs=out_specs, check_vma=False)
```

```python
import functools

import jax
import jax.numpy as jnp
from jax import lax
from jax.experimental import pallas as pl
from jax.experimental.pallas import tpu as pltpu
from jax.sharding import PartitionSpec as P

learn_rate = 0.5
inv_root_two = 0.7071067811865476
inv_root_tau = 0.3989422804014327

VMEM = pl.BlockSpec(memory_space=pltpu.VMEM)
SMEM = pl.BlockSpec(memory_space=pltpu.SMEM)
ANY = pl.BlockSpec(memory_space=pl.ANY)

TP = 4
SLAB = 16


def call(body, outs, in_specs, out_specs=None, scratch=(), flops=0, name=None):
    many = isinstance(outs, (tuple, list))
    listed = outs if many else (outs,)
    size = sum(o.size * o.dtype.itemsize for o in listed)
    return pl.pallas_call(
        body,
        out_shape=outs,
        in_specs=in_specs,
        out_specs=out_specs if out_specs is not None else ([VMEM] * len(listed) if many else VMEM),
        scratch_shapes=list(scratch),
        compiler_params=pltpu.CompilerParams(vmem_limit_bytes=48 * 2**20),
        cost_estimate=pl.CostEstimate(flops=flops, bytes_accessed=3 * size, transcendentals=0),
        name=name,
    )


def dot(left, right, dims):
    return lax.dot_general(left, right, (dims, ((), ())), preferred_element_type=jnp.float32)


def shape(dims, dtype=jnp.bfloat16):
    return jax.ShapeDtypeStruct(dims, dtype)


def cut_body(t_ref, up_ref, down_ref, *rest):
    outs, sem = rest[:-1], rest[-1]
    t = t_ref[0]
    feat = outs[0].shape[1]
    copies = []
    for n, out in enumerate(outs):
        src = up_ref if n < 3 else down_ref
        r = (2, 3, 1)[n % 3]
        cols = pl.ds(pl.multiple_of((t ^ r) * feat, 128), feat)
        copies.append(pltpu.make_async_copy(src.at[:, cols], out, sem.at[n]))
    for copy in copies:
        copy.start()
    for copy in copies:
        copy.wait()


def part_body(t_ref, x_ref, whole_ref, w1_ref, w2_ref, w3_ref, keep_ref, send_ref, cat):
    rows, feat = w1_ref.shape
    cat[0:rows] = whole_ref[:, pl.ds(pl.multiple_of(t_ref[0] * feat, 128), feat)]
    cat[rows : 2 * rows] = w2_ref[...]
    cat[2 * rows : 3 * rows] = w1_ref[...]
    cat[3 * rows :] = w3_ref[...]
    got = dot(cat[...], x_ref[...], ((1,), (1,)))
    keep_ref[...] = got[: 2 * rows]
    send_ref[...] = got[2 * rows :].astype(jnp.bfloat16)


def step_body(scale, t_ref, own_ref, got_ref, y_ref, whole_ref, w1_ref, w2_ref, w3_ref, out_ref, cat):
    rows, feat = w1_ref.shape
    t = t_ref[0]
    cat[: 2 * rows] = own_ref[...]
    cat[2 * rows :] = got_ref[...]
    half = feat // 2
    base = pl.multiple_of(t * feat, 128)
    for fh in range(2):
        grad = dot(cat[...], y_ref[:, fh * half : (fh + 1) * half], ((1,), (0,)))
        for n, r in enumerate((0, 2, 1, 3)):
            if r == 0:
                old = whole_ref[:, pl.ds(pl.multiple_of(base + fh * half, 128), half)]
            else:
                old = (None, w1_ref, w2_ref, w3_ref)[r][:, fh * half : (fh + 1) * half]
            new = old.astype(jnp.float32) - learn_rate * (grad[n * rows : (n + 1) * rows] * scale)
            new = new.astype(jnp.bfloat16)
            for rb in range(rows // SLAB):
                out_ref[(rb * 2 + fh) * TP + (t ^ r)] = new[rb * SLAB : (rb + 1) * SLAB]


def in_grad_body(scale, t_ref, own_ref, got_ref, whole_ref, w1_ref, w2_ref, w3_ref, out_ref, cat, wcat):
    rows, feat = w1_ref.shape
    cat[: 2 * rows] = own_ref[...]
    cat[2 * rows :] = got_ref[...]
    wcat[0:rows] = whole_ref[:, pl.ds(pl.multiple_of(t_ref[0] * feat, 128), feat)]
    wcat[rows : 2 * rows] = w2_ref[...]
    wcat[2 * rows : 3 * rows] = w1_ref[...]
    wcat[3 * rows :] = w3_ref[...]
    got = dot(cat[...], wcat[...], ((0,), (0,)))
    out_ref[...] = (got * scale).astype(jnp.bfloat16)


def member_scales(labels):
    slots = []
    for slot in range(2):
        member = [jnp.where(label == slot, 1.0, 0.0) for label in labels]
        count = functools.reduce(lambda a, b: a + b, member)
        slots.append((member, jnp.maximum(count, 1.0)))
    return slots


def first_body(n_rx, j_ref, gx_ref, up_ref, down_ref, out_ref):
    j = j_ref[0]
    half = up_ref.shape[2] // 2
    slots = member_scales([gx_ref[j, i] for i in range(n_rx)])
    for u, ref in enumerate((up_ref, down_ref)):
        for tt in range(TP):
            for h in range(2):
                cols = slice(h * half, (h + 1) * half)
                sums = [None, None]
                for i in range(n_rx):
                    term = ref[i * TP + tt, :, cols].astype(jnp.float32)
                    for s in range(2):
                        part = term * slots[s][0][i]
                        sums[s] = part if i == 0 else sums[s] + part
                for s in range(2):
                    out_ref[tt * 2 + h, s, u] = (sums[s] / slots[s][1]).astype(jnp.bfloat16)


def second_body(n_rx, n_ry, gx_ref, gy_ref, z_ref, out_ref, pair):
    def line(i, _):
        slots = member_scales([gy_ref[i, k] for k in range(n_ry)])
        for u in range(2):
            sums = [None, None]
            for k in range(n_ry):
                term = z_ref[k, gx_ref[k, i], u].astype(jnp.float32)
                for s in range(2):
                    part = term * slots[s][0][k]
                    sums[s] = part if k == 0 else sums[s] + part
            for s in range(2):
                pair[s, u] = (sums[s] / slots[s][1]).astype(jnp.bfloat16)
        for k in range(n_ry):
            out_ref[i * n_ry + k] = pair[gy_ref[i, k]]
        return 0

    lax.fori_loop(0, n_rx, line, 0)


def last_body(n_rx, n_ry, f_ref, up_ref, down_ref):
    width = f_ref.shape[3]
    feat = up_ref.shape[1] // TP
    for c in range(n_rx):
        rb, fh = c // 2, c % 2
        for m in range(n_ry):
            tt, h = m // 2, m % 2
            at = tt * feat + fh * (feat // 2) + h * width
            for u, ref in enumerate((up_ref, down_ref)):
                ref[rb * SLAB : (rb + 1) * SLAB, at : at + width] = f_ref[c * n_ry + m, u]


def swap(value, r):
    return lax.ppermute(value, "tp", [(t, t ^ r) for t in range(TP)])


def shards(inputs, out_grads, up_weight, down_weight, group_x, group_y):
    x = inputs[0, 0]
    dy = out_grads[0, 0]
    up = up_weight[0, 0]
    down = down_weight[0, 0]
    tok, feat = x.shape
    rows, width = up.shape
    n_rx = lax.axis_size("rx")
    n_ry = lax.axis_size("ry")
    hid = rows * TP
    scale_in = width ** (-0.5)
    scale_hid = hid ** (-0.5)
    t = lax.axis_index("tp").astype(jnp.int32)[None]
    second_pos = lax.axis_index("ry").astype(jnp.int32)[None]
    flops = 2 * tok * feat * hid

    block = shape((rows, feat))
    cuts = call(cut_body, [block] * 6, [SMEM, ANY, ANY], [ANY] * 6, [pltpu.SemaphoreType.DMA((6,))], name="cut")(t, up, down)
    up2, up3, up1 = (swap(cut, r) for cut, r in zip(cuts[:3], (2, 3, 1)))
    down2, down3, down1 = (swap(cut, r) for cut, r in zip(cuts[3:], (2, 3, 1)))
    ups = (up, up1, up2, up3)
    downs = (down, down1, down2, down3)

    def summed(data, weights, name):
        keep, send = call(
            part_body, [shape((2 * rows, tok), jnp.float32), shape((2 * rows, tok))], [SMEM] + [VMEM] * 5,
            scratch=[pltpu.VMEM((hid, feat), jnp.bfloat16)], flops=flops, name=name,
        )(t, data, *weights)
        both = (keep + swap(send, 1).astype(jnp.float32)).astype(jnp.bfloat16)
        far = swap(both, 2).reshape(2, rows, tok)[::-1].reshape(2 * rows, tok)
        return both.astype(jnp.float32) + far.astype(jnp.float32)

    pre = summed(x, ups, "pre_part") * scale_in
    cdf = 0.5 * (1.0 + lax.erf(pre * inv_root_two))
    act = (pre * cdf).astype(jnp.bfloat16)
    slope = cdf + pre * jnp.exp(-0.5 * pre * pre) * inv_root_tau
    act_got = swap(act, 1)
    pieces = n_rx * TP
    cat = pltpu.VMEM((hid, tok), jnp.bfloat16)

    def stepped(scale, own, got, data, weights, name):
        out = call(
            functools.partial(step_body, scale), shape((pieces, SLAB, feat // 2)), [SMEM] + [VMEM] * 7,
            scratch=[cat], flops=flops, name=name,
        )(t, own, got, data, *weights)
        return lax.all_to_all(out, ("rx", "tp"), 0, 0, tiled=True)

    terms_down = stepped(scale_hid, act, act_got, dy, downs, "step_down")
    hid_grad = summed(dy, downs, "hid_part") * scale_hid
    pre_grad = (hid_grad * slope).astype(jnp.bfloat16)
    pre_grad_got = swap(pre_grad, 1)
    terms_up = stepped(scale_in, pre_grad, pre_grad_got, x, ups, "step_up")
    in_grad = call(
        functools.partial(in_grad_body, scale_in), shape((tok, feat)), [SMEM] + [VMEM] * 6,
        scratch=[cat, pltpu.VMEM((hid, feat), jnp.bfloat16)], flops=flops, name="in_grad",
    )(t, pre_grad, pre_grad_got, *ups)

    mids = call(
        functools.partial(first_body, n_rx), shape((n_ry, 2, 2, SLAB, feat // 4)), [SMEM, SMEM, VMEM, VMEM], name="first_round",
    )(second_pos, group_x, terms_up, terms_down)
    mids = lax.all_to_all(mids, "ry", 0, 0, tiled=True)
    news = call(
        functools.partial(second_body, n_rx, n_ry), shape((n_rx * n_ry, 2, SLAB, feat // 4)), [SMEM, SMEM, VMEM],
        scratch=[pltpu.VMEM((2, 2, SLAB, feat // 4), jnp.bfloat16)], name="second_round",
    )(group_x, group_y, mids)
    news = lax.all_to_all(news, ("rx", "ry"), 0, 0, tiled=True)
    new_up, new_down = call(
        functools.partial(last_body, n_rx, n_ry), [shape((rows, width))] * 2, [VMEM], name="last",
    )(news)
    return (in_grad[None, None], new_up[None, None], new_down[None, None])


def solution(mesh):
    in_specs = (
        P("rx", "ry", None, "tp"),
        P("rx", "ry", None, "tp"),
        P("rx", "ry", "tp", None),
        P("rx", "ry", "tp", None),
        P(),
        P(),
    )
    out_specs = (P("rx", "ry", None, "tp"), P("rx", "ry", "tp", None), P("rx", "ry", "tp", None))
    return jax.shard_map(shards, mesh=mesh, in_specs=in_specs, out_specs=out_specs, check_vma=False)
```

```python
import functools

import jax
import jax.numpy as jnp
from jax import lax
from jax.experimental import pallas as pl
from jax.experimental.pallas import tpu as pltpu
from jax.sharding import PartitionSpec as P

learn_rate = 0.5
inv_root_two = 0.7071067811865476
inv_root_tau = 0.3989422804014327

ANY = pl.BlockSpec(memory_space=pl.ANY)
SMEM = pl.BlockSpec(memory_space=pltpu.SMEM)
VMEM = pl.BlockSpec(memory_space=pltpu.VMEM)

TP = 4
SLAB = 16


def shape(dims, dtype=jnp.bfloat16):
    return jax.ShapeDtypeStruct(dims, dtype)


def vmem(dims, dtype=jnp.bfloat16):
    return pltpu.VMEM(dims, dtype)


def call(body, outs, args, specs, scratch=(), out_specs=None, alias=None, flops=0, name=None):
    kinds = {"s": SMEM, "v": VMEM, "a": ANY}
    size = sum(a.size * a.dtype.itemsize for a in list(outs) + list(args))
    return pl.pallas_call(
        body,
        out_shape=list(outs),
        in_specs=[kinds[c] for c in specs],
        out_specs=[kinds[c] for c in out_specs or "v" * len(outs)],
        scratch_shapes=list(scratch),
        input_output_aliases={} if alias is None else {alias: 0},
        compiler_params=pltpu.CompilerParams(vmem_limit_bytes=24 * 2**20),
        cost_estimate=pl.CostEstimate(flops=flops, bytes_accessed=size, transcendentals=0),
        name=name,
    )(*args)


def dot(left, right, dims):
    return lax.dot_general(left, right, (dims, ((), ())), preferred_element_type=jnp.float32)


ORDER = (0, 2, 1, 3)


def cut_body(pos_ref, weight_ref, *rest):
    outs, sems = rest[-5:-1], rest[-1]
    feat = outs[0].shape[1]
    copies = []
    for n, r in enumerate((2, 3, 1, 0)):
        cols = pl.ds(pl.multiple_of((pos_ref[0] ^ r) * feat, 128), feat)
        copies.append(pltpu.make_async_copy(weight_ref.at[:, cols], outs[n], sems.at[n]))
    for copy in copies:
        copy.start()
    for copy in copies:
        copy.wait()


def part_body(x_ref, w0, w1, w2, w3, *rest):
    keep_ref, send_ref, w_ref = rest[-3:]
    rows = w0.shape[0]
    for n, r in enumerate(ORDER):
        w_ref[n * rows : (n + 1) * rows] = (w0, w1, w2, w3)[r][...]
    got = dot(w_ref[...], x_ref[...], ((1,), (1,)))
    half = keep_ref.shape[0]
    keep_ref[...] = got[:half]
    send_ref[...] = got[half:].astype(jnp.bfloat16)


def pair_body(keep_ref, got_ref, both_ref):
    both_ref[...] = (keep_ref[...] + got_ref[...].astype(jnp.float32)).astype(jnp.bfloat16)


def far_sum(both_ref, far_ref):
    rows = both_ref.shape[0] // 2
    far = far_ref[...].astype(jnp.float32)
    return both_ref[...].astype(jnp.float32) + jnp.concatenate([far[rows:], far[:rows]], axis=0)


def act_body(scale, both_ref, far_ref, act_ref, slope_ref):
    pre = far_sum(both_ref, far_ref) * scale
    cdf = 0.5 * (1.0 + lax.erf(pre * inv_root_two))
    act_ref[...] = (pre * cdf).astype(jnp.bfloat16)
    slope_ref[...] = cdf + pre * jnp.exp(-0.5 * pre * pre) * inv_root_tau


def pre_grad_body(scale, both_ref, far_ref, slope_ref, out_ref):
    out_ref[...] = (far_sum(both_ref, far_ref) * scale * slope_ref[...]).astype(jnp.bfloat16)


def step_body(scale, u, pos_ref, own_ref, got_ref, y_ref, w_ref, *rest):
    out_ref, cat, new, sems = rest[-4:]
    half_hid = own_ref.shape[0]
    hid, feat = w_ref.shape
    cat[:half_hid] = own_ref[...]
    cat[half_hid:] = got_ref[...]
    half = feat // 2
    copies = []
    for fh in range(2):
        c = slice(fh * half, (fh + 1) * half)
        grad = dot(cat[...], y_ref[:, c], ((1,), (0,)))
        step = (w_ref[:, c].astype(jnp.float32) - learn_rate * (grad * scale)).astype(jnp.bfloat16)
        new[fh] = step.reshape(new.shape[1:])
        for n, r in enumerate(ORDER):
            copy = pltpu.make_async_copy(new.at[fh, n], out_ref.at[:, fh, pos_ref[0] ^ r, u], sems.at[len(copies)])
            copy.start()
            copies.append(copy)
    for copy in copies:
        copy.wait()


def in_grad_body(scale, own_ref, got_ref, w_ref, out_ref, cat):
    half_hid = own_ref.shape[0]
    cat[:half_hid] = own_ref[...]
    cat[half_hid:] = got_ref[...]
    out_ref[...] = (dot(cat[...], w_ref[...], ((0,), (0,))) * scale).astype(jnp.bfloat16)


def total(values):
    return functools.reduce(lambda a, b: a + b, values)


def members_of(labels):
    members = [[jnp.where(label == s, 1.0, 0.0) for label in labels] for s in range(2)]
    return [(member, jnp.maximum(total(member), 1.0)) for member in members]


def first_body(n_rx, pos_ref, gx_ref, terms_ref, *outs):
    k = pos_ref[2]
    slots = members_of([gx_ref[k, i] for i in range(n_rx)])
    for q, out in enumerate(outs):
        part = lax.rem(k + q, TP)
        for u in range(2):
            values = [terms_ref[i * TP + part, u].astype(jnp.float32) for i in range(n_rx)]
            for s, (member, count) in enumerate(slots):
                out[s, u] = (total(value * one for value, one in zip(values, member)) / count).astype(jnp.bfloat16)


def second_body(u, n_ry, pos_ref, gx_ref, gy_ref, *rest):
    mids, out_ref = rest[:n_ry], rest[-1]
    places = [lax.rem(pos_ref[2] + (n_ry - s), n_ry) for s in range(n_ry)]

    def line(i, _):
        slots = members_of([gy_ref[i, place] for place in places])
        values = [mid[gx_ref[place, i], u].astype(jnp.float32) for mid, place in zip(mids, places)]
        for s, (member, count) in enumerate(slots):
            mean = total(value * one for value, one in zip(values, member)) / count
            out_ref[i, s] = mean.astype(jnp.bfloat16)
        return 0

    lax.fori_loop(0, out_ref.shape[0], line, 0)


def pick_body(n_rx, n_ry, pos_ref, gy_ref, both_ref, *outs):
    i, k = pos_ref[1], pos_ref[2]
    far = jnp.where(lax.rem(k, 2) == 0, n_ry - 2, 2)
    for out, shift in zip(outs, (0, 1, n_ry - 1, far)):
        label = gy_ref[i, lax.rem(k + shift, n_ry)]
        for c in range(n_rx):
            out[c] = both_ref[c, label]


def last_body(n_rx, pos_ref, own_ref, before_ref, after_ref, far_ref, out_ref):
    k = pos_ref[2]
    width = own_ref.shape[2]
    for q, ref in ((0, own_ref), (TP - 1, before_ref), (1, after_ref), (2, far_ref)):
        m = lax.rem(k + q, TP)
        for c in range(n_rx):
            rb, fh = c // 2, c % 2
            cols = pl.ds(pl.multiple_of(m * (2 * width) + fh * width, 128), width)
            out_ref[rb * SLAB : (rb + 1) * SLAB, cols] = ref[c]


def swap(value, r):
    return lax.ppermute(value, "tp", [(t, t ^ r) for t in range(TP)])


def shards(inputs, out_grads, up_weight, down_weight, group_x, group_y):
    x = inputs[0, 0]
    dy = out_grads[0, 0]
    tok, feat = x.shape
    rows, width = up_weight.shape[2:]
    n_rx = lax.axis_size("rx")
    n_ry = lax.axis_size("ry")
    hid = rows * TP
    scale_in = width ** (-0.5)
    scale_hid = hid ** (-0.5)
    pos = jnp.stack([lax.axis_index("tp"), lax.axis_index("rx"), lax.axis_index("ry")]).astype(jnp.int32)
    flops = 2 * tok * feat * hid
    half, half_wide = shape((2 * rows, tok)), shape((2 * rows, tok), jnp.float32)
    cat = vmem((hid, tok))

    def spread(weight, after, name):
        two, three, one, own = call(
            cut_body, [shape((rows, feat))] * TP, [pos, weight, *after], "sa" + "a" * len(after),
            [pltpu.SemaphoreType.DMA((TP,))], "aaaa", name=name,
        )
        two, three, one = swap(two, 2), swap(three, 3), swap(one, 1)
        return [own, one, two, three]

    ups = spread(up_weight[0, 0], [], "cut_up")
    downs = spread(down_weight[0, 0], [ups[1]], "cut_down")

    def summed(data, weights, after, name):
        keep, send, stacked = call(
            part_body, [half_wide, half, shape((hid, feat))], [data, *weights, *after], "vvvvv" + "a" * len(after),
            flops=flops, name="part_" + name,
        )
        (both,) = call(pair_body, [half], [keep, swap(send, 1)], "vv", name="pair_" + name)
        return both, swap(both, 2), stacked

    both, far, up = summed(x, ups, [], "pre")
    act, slope = call(functools.partial(act_body, scale_in), [half, half_wide], [both, far], "vv", name="act")
    act_got = swap(act, 1)
    both, far, down = summed(dy, downs, [both], "hid")
    (pre_grad,) = call(functools.partial(pre_grad_body, scale_hid), [half], [both, far, slope], "vvv", name="pre_grad")
    pre_grad_got = swap(pre_grad, 1)

    def stepped(scale, u, own, got, data, weight, filled, name):
        (out,) = call(
            functools.partial(step_body, scale, u), [shape((n_rx // 2, 2, TP, 2, SLAB, feat // 2))],
            [pos, own, got, data, weight, *filled], "svvvv" + "a" * len(filled),
            [cat, vmem((2, TP, rows // SLAB, SLAB, feat // 2)), pltpu.SemaphoreType.DMA((2 * TP,))], "a",
            alias=5 if filled else None, flops=flops, name=name,
        )
        return out

    steps = stepped(scale_hid, 0, act, act_got, dy, down, [], "step_down")
    steps = stepped(scale_in, 1, pre_grad, pre_grad_got, x, up, [steps], "step_up")
    (in_grad,) = call(
        functools.partial(in_grad_body, scale_in), [shape((tok, feat))], [pre_grad, pre_grad_got, up], "vvv", [cat], flops=flops, name="in_grad"
    )

    terms = lax.all_to_all(steps.reshape(n_rx * TP, 2, SLAB, feat // 2), ("rx", "tp"), 0, 0, tiled=True)
    def along(value, shift):
        return lax.ppermute(value, "ry", [(k, (k + shift) % n_ry) for k in range(n_ry)])

    def two_away(value):
        return lax.ppermute(value, "ry", [(k, (k + (2 if k % 2 else n_ry - 2)) % n_ry) for k in range(n_ry)])

    parts = call(
        functools.partial(first_body, n_rx), [shape((2, 2, SLAB, feat // 2))] * TP, [pos, group_x, terms], "ssv", name="first_round"
    )
    mids = [parts[0]] + [None] * (n_ry - 1)
    for s in (4, 3, 5, 2, 6, 1, 7):
        mids[s] = along(parts[s % TP], s)

    def averaged(u, name):
        (news,) = call(
            functools.partial(second_body, u, n_ry), [shape((n_rx, 2, SLAB, feat // 2))], [pos, group_x, group_y, *mids],
            "sss" + "v" * n_ry, name="second_" + name,
        )
        news = lax.all_to_all(news, "rx", 0, 0, tiled=True)
        own, after, before, far = call(
            functools.partial(pick_body, n_rx, n_ry), [shape((n_rx, SLAB, feat // 2))] * 4, [pos, group_y, news], "ssv", name="pick_" + name
        )
        held = [own, along(after, 1), along(before, -1), two_away(far)]
        (out,) = call(functools.partial(last_body, n_rx), [shape((rows, width))], [pos, *held], "svvvv", name="last_" + name)
        return out

    new_down = averaged(0, "down")
    new_up = averaged(1, "up")
    return (in_grad[None, None], new_up[None, None], new_down[None, None])


def solution(mesh):
    in_specs = (
        P("rx", "ry", None, "tp"),
        P("rx", "ry", None, "tp"),
        P("rx", "ry", "tp", None),
        P("rx", "ry", "tp", None),
        P(),
        P(),
    )
    out_specs = (P("rx", "ry", None, "tp"), P("rx", "ry", "tp", None), P("rx", "ry", "tp", None))
    return jax.shard_map(shards, mesh=mesh, in_specs=in_specs, out_specs=out_specs, check_vma=False)
```

```python
import functools

import jax
import jax.numpy as jnp
from jax import lax
from jax.experimental import pallas as pl
from jax.experimental.pallas import tpu as pltpu
from jax.sharding import PartitionSpec as P

learn_rate = 0.5
inv_root_two = 0.7071067811865476
inv_root_tau = 0.3989422804014327

ANY = pl.BlockSpec(memory_space=pl.ANY)
SMEM = pl.BlockSpec(memory_space=pltpu.SMEM)
VMEM = pl.BlockSpec(memory_space=pltpu.VMEM)

TP = 4
SHIFTS = (0, 1, 7, 2, 6, 3, 5, 4)
SLAB = 16


def shape(dims, dtype=jnp.bfloat16):
    return jax.ShapeDtypeStruct(dims, dtype)


def vmem(dims, dtype=jnp.bfloat16):
    return pltpu.VMEM(dims, dtype)


def call(body, outs, args, specs, scratch=(), out_specs=None, alias=None, flops=0, name=None):
    kinds = {"s": SMEM, "v": VMEM, "a": ANY}
    size = sum(a.size * a.dtype.itemsize for a in list(outs) + list(args))
    return pl.pallas_call(
        body,
        out_shape=list(outs),
        in_specs=[kinds[c] for c in specs],
        out_specs=[kinds[c] for c in out_specs or "v" * len(outs)],
        scratch_shapes=list(scratch),
        input_output_aliases={} if alias is None else {alias: 0},
        compiler_params=pltpu.CompilerParams(vmem_limit_bytes=24 * 2**20),
        cost_estimate=pl.CostEstimate(flops=flops, bytes_accessed=size, transcendentals=0),
        name=name,
    )(*args)


def dot(left, right, dims):
    return lax.dot_general(left, right, (dims, ((), ())), preferred_element_type=jnp.float32)


ORDER = (0, 2, 1, 3)


def cut_body(pos_ref, weight_ref, *rest):
    outs, sems = rest[-5:-1], rest[-1]
    feat = outs[0].shape[1]
    copies = []
    for n, r in enumerate((2, 3, 1, 0)):
        cols = pl.ds(pl.multiple_of((pos_ref[0] ^ r) * feat, 128), feat)
        copies.append(pltpu.make_async_copy(weight_ref.at[:, cols], outs[n], sems.at[n]))
    for copy in copies:
        copy.start()
    for copy in copies:
        copy.wait()


def part_body(x_ref, w0, w1, w2, w3, *rest):
    keep_ref, send_ref, w_ref = rest[-3:]
    rows = w0.shape[0]
    for n, r in enumerate(ORDER):
        w_ref[n * rows : (n + 1) * rows] = (w0, w1, w2, w3)[r][...]
    got = dot(w_ref[...], x_ref[...], ((1,), (1,)))
    half = keep_ref.shape[0]
    keep_ref[...] = got[:half]
    send_ref[...] = got[half:].astype(jnp.bfloat16)


def pair_body(keep_ref, got_ref, both_ref):
    both_ref[...] = (keep_ref[...] + got_ref[...].astype(jnp.float32)).astype(jnp.bfloat16)


def far_sum(both_ref, far_ref):
    rows = both_ref.shape[0] // 2
    far = far_ref[...].astype(jnp.float32)
    return both_ref[...].astype(jnp.float32) + jnp.concatenate([far[rows:], far[:rows]], axis=0)


def act_body(scale, both_ref, far_ref, act_ref, slope_ref):
    pre = far_sum(both_ref, far_ref) * scale
    cdf = 0.5 * (1.0 + lax.erf(pre * inv_root_two))
    act_ref[...] = (pre * cdf).astype(jnp.bfloat16)
    slope_ref[...] = cdf + pre * jnp.exp(-0.5 * pre * pre) * inv_root_tau


def pre_grad_body(scale, both_ref, far_ref, slope_ref, out_ref):
    out_ref[...] = (far_sum(both_ref, far_ref) * scale * slope_ref[...]).astype(jnp.bfloat16)


def step_body(scale, u, pos_ref, own_ref, got_ref, y_ref, w_ref, *rest):
    out_ref, cat, new, sems = rest[-4:]
    half_hid = own_ref.shape[0]
    hid, feat = w_ref.shape
    cat[:half_hid] = own_ref[...]
    cat[half_hid:] = got_ref[...]
    half = feat // 2
    copies = []
    for fh in range(2):
        c = slice(fh * half, (fh + 1) * half)
        grad = dot(cat[...], y_ref[:, c], ((1,), (0,)))
        step = (w_ref[:, c].astype(jnp.float32) - learn_rate * (grad * scale)).astype(jnp.bfloat16)
        new[fh] = step.reshape(new.shape[1:])
        for n, r in enumerate(ORDER):
            copy = pltpu.make_async_copy(new.at[fh, n], out_ref.at[:, fh, pos_ref[0] ^ r, u], sems.at[len(copies)])
            copy.start()
            copies.append(copy)
    for copy in copies:
        copy.wait()


def in_grad_body(scale, own_ref, got_ref, w_ref, out_ref, cat):
    half_hid = own_ref.shape[0]
    cat[:half_hid] = own_ref[...]
    cat[half_hid:] = got_ref[...]
    out_ref[...] = (dot(cat[...], w_ref[...], ((0,), (0,))) * scale).astype(jnp.bfloat16)


def total(values):
    return functools.reduce(lambda a, b: a + b, values)


def members_of(labels):
    members = [[jnp.where(label == s, 1.0, 0.0) for label in labels] for s in range(2)]
    return [(member, 1.0 / jnp.maximum(total(member), 1.0)) for member in members]


def group_means(terms, slots):
    sums = [None, None]
    for n, term in enumerate(terms):
        term = term.astype(jnp.float32)
        for s, (member, _) in enumerate(slots):
            part = term * member[n]
            sums[s] = part if n == 0 else sums[s] + part
    return [(value * share).astype(jnp.bfloat16) for value, (_, share) in zip(sums, slots)]


def first_body(n_rx, pos_ref, gx_ref, terms_ref, *outs):
    k = pos_ref[2]
    slots = members_of([gx_ref[k, i] for i in range(n_rx)])
    for q in range(TP):
        part = lax.rem(k + q, TP)
        for u in range(2):
            for s, mean in enumerate(group_means((terms_ref[i * TP + part, u] for i in range(n_rx)), slots)):
                for shift in range(q, len(outs), TP):
                    outs[SHIFTS.index(shift)][s, u] = mean


def second_body(u, n_ry, pos_ref, gx_ref, gy_ref, *rest):
    mids, out_ref = rest[:n_ry], rest[-1]
    places = [lax.rem(pos_ref[2] + (n_ry - s), n_ry) for s in SHIFTS]

    def line(i, _):
        slots = members_of([gy_ref[i, place] for place in places])
        for s, mean in enumerate(group_means((mid[gx_ref[place, i], u] for mid, place in zip(mids, places)), slots)):
            out_ref[i, s] = mean
        return 0

    lax.fori_loop(0, out_ref.shape[0], line, 0)


def pick_body(n_rx, n_ry, pos_ref, gy_ref, both_ref, *outs):
    i, k = pos_ref[1], pos_ref[2]
    far = jnp.where(lax.rem(k, 2) == 0, n_ry - 2, 2)
    for out, shift in zip(outs, (0, 1, n_ry - 1, far)):
        label = gy_ref[i, lax.rem(k + shift, n_ry)]
        for c in range(n_rx):
            out[c] = both_ref[c, label]


def last_body(n_rx, pos_ref, own_ref, before_ref, after_ref, far_ref, out_ref):
    k = pos_ref[2]
    width = own_ref.shape[2]
    for q, ref in ((0, own_ref), (TP - 1, before_ref), (1, after_ref), (2, far_ref)):
        m = lax.rem(k + q, TP)
        for c in range(n_rx):
            rb, fh = c // 2, c % 2
            cols = pl.ds(pl.multiple_of(m * (2 * width) + fh * width, 128), width)
            out_ref[rb * SLAB : (rb + 1) * SLAB, cols] = ref[c]


def swap(value, r):
    return lax.ppermute(value, "tp", [(t, t ^ r) for t in range(TP)])


def shards(inputs, out_grads, up_weight, down_weight, group_x, group_y):
    x = inputs[0, 0]
    dy = out_grads[0, 0]
    tok, feat = x.shape
    rows, width = up_weight.shape[2:]
    n_rx = lax.axis_size("rx")
    n_ry = lax.axis_size("ry")
    hid = rows * TP
    scale_in = width ** (-0.5)
    scale_hid = hid ** (-0.5)
    pos = jnp.stack([lax.axis_index("tp"), lax.axis_index("rx"), lax.axis_index("ry")]).astype(jnp.int32)
    flops = 2 * tok * feat * hid
    half, half_wide = shape((2 * rows, tok)), shape((2 * rows, tok), jnp.float32)
    cat = vmem((hid, tok))

    def spread(weight, after, name):
        two, three, one, own = call(
            cut_body, [shape((rows, feat))] * TP, [pos, weight, *after], "sa" + "a" * len(after),
            [pltpu.SemaphoreType.DMA((TP,))], "aaaa", name=name,
        )
        two, three, one = swap(two, 2), swap(three, 3), swap(one, 1)
        return [own, one, two, three]

    ups = spread(up_weight[0, 0], [], "cut_up")
    downs = spread(down_weight[0, 0], [ups[1]], "cut_down")

    def summed(data, weights, after, name):
        keep, send, stacked = call(
            part_body, [half_wide, half, shape((hid, feat))], [data, *weights, *after], "vvvvv" + "a" * len(after),
            flops=flops, name="part_" + name,
        )
        (both,) = call(pair_body, [half], [keep, swap(send, 1)], "vv", name="pair_" + name)
        return both, swap(both, 2), stacked

    both, far, up = summed(x, ups, [], "pre")
    act, slope = call(functools.partial(act_body, scale_in), [half, half_wide], [both, far], "vv", name="act")
    act_got = swap(act, 1)
    both, far, down = summed(dy, downs, [both], "hid")
    (pre_grad,) = call(functools.partial(pre_grad_body, scale_hid), [half], [both, far, slope], "vvv", name="pre_grad")
    pre_grad_got = swap(pre_grad, 1)

    def stepped(scale, u, own, got, data, weight, filled, name):
        (out,) = call(
            functools.partial(step_body, scale, u), [shape((n_rx // 2, 2, TP, 2, SLAB, feat // 2))],
            [pos, own, got, data, weight, *filled], "svvvv" + "a" * len(filled),
            [cat, vmem((2, TP, rows // SLAB, SLAB, feat // 2)), pltpu.SemaphoreType.DMA((2 * TP,))], "a",
            alias=5 if filled else None, flops=flops, name=name,
        )
        return out

    steps = stepped(scale_hid, 0, act, act_got, dy, down, [], "step_down")
    steps = stepped(scale_in, 1, pre_grad, pre_grad_got, x, up, [steps], "step_up")
    (in_grad,) = call(
        functools.partial(in_grad_body, scale_in), [shape((tok, feat))], [pre_grad, pre_grad_got, up], "vvv", [cat], flops=flops, name="in_grad"
    )

    terms = lax.all_to_all(steps.reshape(n_rx * TP, 2, SLAB, feat // 2), ("rx", "tp"), 0, 0, tiled=True)
    def along(value, shift):
        return lax.ppermute(value, "ry", [(k, (k + shift) % n_ry) for k in range(n_ry)])

    def two_away(value):
        return lax.ppermute(value, "ry", [(k, (k + (2 if k % 2 else n_ry - 2)) % n_ry) for k in range(n_ry)])

    parts = call(
        functools.partial(first_body, n_rx), [shape((2, 2, SLAB, feat // 2))] * n_ry, [pos, group_x, terms], "ssv", name="first_round"
    )
    mids = [along(part, s) if s else part for s, part in zip(SHIFTS, parts)]

    def averaged(u, name):
        (news,) = call(
            functools.partial(second_body, u, n_ry), [shape((n_rx, 2, SLAB, feat // 2))], [pos, group_x, group_y, *mids],
            "sss" + "v" * n_ry, name="second_" + name,
        )
        news = lax.all_to_all(news, "rx", 0, 0, tiled=True)
        own, after, before, far = call(
            functools.partial(pick_body, n_rx, n_ry), [shape((n_rx, SLAB, feat // 2))] * 4, [pos, group_y, news], "ssv", name="pick_" + name
        )
        held = [own, along(after, 1), along(before, -1), two_away(far)]
        (out,) = call(functools.partial(last_body, n_rx), [shape((rows, width))], [pos, *held], "svvvv", name="last_" + name)
        return out

    new_down = averaged(0, "down")
    new_up = averaged(1, "up")
    return (in_grad[None, None], new_up[None, None], new_down[None, None])


def solution(mesh):
    in_specs = (
        P("rx", "ry", None, "tp"),
        P("rx", "ry", None, "tp"),
        P("rx", "ry", "tp", None),
        P("rx", "ry", "tp", None),
        P(),
        P(),
    )
    out_specs = (P("rx", "ry", None, "tp"), P("rx", "ry", "tp", None), P("rx", "ry", "tp", None))
    return jax.shard_map(shards, mesh=mesh, in_specs=in_specs, out_specs=out_specs, check_vma=False)
```

```python
import functools

import jax
import jax.numpy as jnp
from jax import lax
from jax.experimental import pallas as pl
from jax.experimental.pallas import tpu as pltpu
from jax.sharding import PartitionSpec as P

learn_rate = 0.5
inv_root_two = 0.7071067811865476
inv_root_tau = 0.3989422804014327

ANY = pl.BlockSpec(memory_space=pl.ANY)
SMEM = pl.BlockSpec(memory_space=pltpu.SMEM)
VMEM = pl.BlockSpec(memory_space=pltpu.VMEM)

TP = 4
SHIFTS = (0, 1, 7, 2, 6, 3, 5, 4)
SLAB = 16


def shape(dims, dtype=jnp.bfloat16):
    return jax.ShapeDtypeStruct(dims, dtype)


def vmem(dims, dtype=jnp.bfloat16):
    return pltpu.VMEM(dims, dtype)


def call(body, outs, args, specs, scratch=(), out_specs=None, alias=None, flops=0, name=None):
    kinds = {"s": SMEM, "v": VMEM, "a": ANY}
    size = sum(a.size * a.dtype.itemsize for a in list(outs) + list(args))
    return pl.pallas_call(
        body,
        out_shape=list(outs),
        in_specs=[kinds[c] for c in specs],
        out_specs=[kinds[c] for c in out_specs or "v" * len(outs)],
        scratch_shapes=list(scratch),
        input_output_aliases={} if alias is None else {alias: 0},
        compiler_params=pltpu.CompilerParams(vmem_limit_bytes=24 * 2**20),
        cost_estimate=pl.CostEstimate(flops=flops, bytes_accessed=size, transcendentals=0),
        name=name,
    )(*args)


def dot(left, right, dims):
    return lax.dot_general(left, right, (dims, ((), ())), preferred_element_type=jnp.float32)


ORDER = (0, 2, 1, 3)


def cut_body(pos_ref, weight_ref, *rest):
    outs, sems = rest[-5:-1], rest[-1]
    feat = outs[0].shape[1]
    copies = []
    for n, r in enumerate((2, 3, 1, 0)):
        cols = pl.ds(pl.multiple_of((pos_ref[0] ^ r) * feat, 128), feat)
        copies.append(pltpu.make_async_copy(weight_ref.at[:, cols], outs[n], sems.at[n]))
    for copy in copies:
        copy.start()
    for copy in copies:
        copy.wait()


def part_body(x_ref, w0, w1, w2, w3, *rest):
    keep_ref, send_ref, w_ref = rest[-3:]
    rows = w0.shape[0]
    for n, r in enumerate(ORDER):
        w_ref[n * rows : (n + 1) * rows] = (w0, w1, w2, w3)[r][...]
    got = dot(w_ref[...], x_ref[...], ((1,), (1,)))
    half = keep_ref.shape[0]
    keep_ref[...] = got[:half]
    send_ref[...] = got[half:].astype(jnp.bfloat16)


def pair_body(keep_ref, got_ref, both_ref):
    both_ref[...] = (keep_ref[...] + got_ref[...].astype(jnp.float32)).astype(jnp.bfloat16)


def far_sum(both_ref, far_ref):
    rows = both_ref.shape[0] // 2
    far = far_ref[...].astype(jnp.float32)
    return both_ref[...].astype(jnp.float32) + jnp.concatenate([far[rows:], far[:rows]], axis=0)


def act_body(scale, both_ref, far_ref, act_ref, slope_ref):
    pre = far_sum(both_ref, far_ref) * scale
    cdf = 0.5 * (1.0 + lax.erf(pre * inv_root_two))
    act_ref[...] = (pre * cdf).astype(jnp.bfloat16)
    slope_ref[...] = cdf + pre * jnp.exp(-0.5 * pre * pre) * inv_root_tau


def pre_grad_body(scale, both_ref, far_ref, slope_ref, out_ref):
    out_ref[...] = (far_sum(both_ref, far_ref) * scale * slope_ref[...]).astype(jnp.bfloat16)


def step_body(scale, u, pos_ref, own_ref, got_ref, y_ref, w_ref, *rest):
    out_ref, cat, new, sems = rest[-4:]
    half_hid = own_ref.shape[0]
    hid, feat = w_ref.shape
    cat[:half_hid] = own_ref[...]
    cat[half_hid:] = got_ref[...]
    half = feat // 2
    copies = []
    for fh in range(2):
        c = slice(fh * half, (fh + 1) * half)
        grad = dot(cat[...], y_ref[:, c], ((1,), (0,)))
        step = (w_ref[:, c].astype(jnp.float32) - learn_rate * (grad * scale)).astype(jnp.bfloat16)
        new[fh] = step.reshape(new.shape[1:])
        for n, r in enumerate(ORDER):
            copy = pltpu.make_async_copy(new.at[fh, n], out_ref.at[:, fh, pos_ref[0] ^ r, u], sems.at[len(copies)])
            copy.start()
            copies.append(copy)
    for copy in copies:
        copy.wait()


def in_grad_body(scale, own_ref, got_ref, w_ref, out_ref, cat):
    half_hid = own_ref.shape[0]
    cat[:half_hid] = own_ref[...]
    cat[half_hid:] = got_ref[...]
    out_ref[...] = (dot(cat[...], w_ref[...], ((0,), (0,))) * scale).astype(jnp.bfloat16)


def total(values):
    return functools.reduce(lambda a, b: a + b, values)


def members_of(labels):
    members = [[jnp.where(label == s, 1.0, 0.0) for label in labels] for s in range(2)]
    return [(member, 1.0 / jnp.maximum(total(member), 1.0)) for member in members]


def group_means(terms, slots):
    sums = [None, None]
    for n, term in enumerate(terms):
        term = term.astype(jnp.float32)
        for s, (member, _) in enumerate(slots):
            part = term * member[n]
            sums[s] = part if n == 0 else sums[s] + part
    return [(value * share).astype(jnp.bfloat16) for value, (_, share) in zip(sums, slots)]


def first_body(n_rx, pos_ref, gx_ref, terms_ref, *outs):
    k = pos_ref[2]
    slots = members_of([gx_ref[k, i] for i in range(n_rx)])
    for q in range(TP):
        part = lax.rem(k + q, TP)
        for u in range(2):
            for s, mean in enumerate(group_means((terms_ref[i * TP + part, u] for i in range(n_rx)), slots)):
                for shift in range(q, len(outs), TP):
                    outs[SHIFTS.index(shift)][s, u] = mean


def second_body(u, n_ry, pos_ref, gx_ref, gy_ref, *rest):
    mids, out_ref = rest[:n_ry], rest[-1]
    places = [lax.rem(pos_ref[2] + (n_ry - s), n_ry) for s in SHIFTS]

    def line(i, _):
        slots = members_of([gy_ref[i, place] for place in places])
        for s, mean in enumerate(group_means((mid[gx_ref[place, i], u] for mid, place in zip(mids, places)), slots)):
            out_ref[i, s] = mean
        return 0

    lax.fori_loop(0, out_ref.shape[0], line, 0)


def pick_body(n_rx, n_ry, pos_ref, gy_ref, both_ref, *outs):
    i, k = pos_ref[1], pos_ref[2]
    far = jnp.where(lax.rem(k, 2) == 0, n_ry - 2, 2)
    for out, shift in zip(outs, (0, 1, n_ry - 1, far)):
        label = gy_ref[i, lax.rem(k + shift, n_ry)]
        for c in range(n_rx):
            out[c] = both_ref[c, label]


def last_body(n_rx, pos_ref, own_ref, far_ref, before_ref, after_ref, out_ref):
    k = pos_ref[2]
    width = own_ref.shape[2]
    for q, ref in ((0, own_ref), (TP - 1, before_ref), (1, after_ref), (2, far_ref)):
        m = lax.rem(k + q, TP)
        for c in range(n_rx):
            rb, fh = c // 2, c % 2
            cols = pl.ds(pl.multiple_of(m * (2 * width) + fh * width, 128), width)
            out_ref[rb * SLAB : (rb + 1) * SLAB, cols] = ref[c]


def swap(value, r):
    return lax.ppermute(value, "tp", [(t, t ^ r) for t in range(TP)])


def shards(inputs, out_grads, up_weight, down_weight, group_x, group_y):
    x = inputs[0, 0]
    dy = out_grads[0, 0]
    tok, feat = x.shape
    rows, width = up_weight.shape[2:]
    n_rx = lax.axis_size("rx")
    n_ry = lax.axis_size("ry")
    hid = rows * TP
    scale_in = width ** (-0.5)
    scale_hid = hid ** (-0.5)
    pos = jnp.stack([lax.axis_index("tp"), lax.axis_index("rx"), lax.axis_index("ry")]).astype(jnp.int32)
    flops = 2 * tok * feat * hid
    half, half_wide = shape((2 * rows, tok)), shape((2 * rows, tok), jnp.float32)
    cat = vmem((hid, tok))

    def spread(weight, after, name):
        two, three, one, own = call(
            cut_body, [shape((rows, feat))] * TP, [pos, weight, *after], "sa" + "a" * len(after),
            [pltpu.SemaphoreType.DMA((TP,))], "aaaa", name=name,
        )
        two, three, one = swap(two, 2), swap(three, 3), swap(one, 1)
        return [own, one, two, three]

    ups = spread(up_weight[0, 0], [], "cut_up")
    downs = spread(down_weight[0, 0], [ups[1]], "cut_down")

    def summed(data, weights, after, name):
        keep, send, stacked = call(
            part_body, [half_wide, half, shape((hid, feat))], [data, *weights, *after], "vvvvv" + "a" * len(after),
            flops=flops, name="part_" + name,
        )
        (both,) = call(pair_body, [half], [keep, swap(send, 1)], "vv", name="pair_" + name)
        return both, swap(both, 2), stacked

    both, far, up = summed(x, ups, [], "pre")
    act, slope = call(functools.partial(act_body, scale_in), [half, half_wide], [both, far], "vv", name="act")
    act_got = swap(act, 1)
    both, far, down = summed(dy, downs, [both], "hid")
    (pre_grad,) = call(functools.partial(pre_grad_body, scale_hid), [half], [both, far, slope], "vvv", name="pre_grad")
    pre_grad_got = swap(pre_grad, 1)

    def stepped(scale, u, own, got, data, weight, filled, name):
        (out,) = call(
            functools.partial(step_body, scale, u), [shape((n_rx // 2, 2, TP, 2, SLAB, feat // 2))],
            [pos, own, got, data, weight, *filled], "svvvv" + "a" * len(filled),
            [cat, vmem((2, TP, rows // SLAB, SLAB, feat // 2)), pltpu.SemaphoreType.DMA((2 * TP,))], "a",
            alias=5 if filled else None, flops=flops, name=name,
        )
        return out

    steps = stepped(scale_hid, 0, act, act_got, dy, down, [], "step_down")
    steps = stepped(scale_in, 1, pre_grad, pre_grad_got, x, up, [steps], "step_up")
    (in_grad,) = call(
        functools.partial(in_grad_body, scale_in), [shape((tok, feat))], [pre_grad, pre_grad_got, up], "vvv", [cat], flops=flops, name="in_grad"
    )

    terms = lax.all_to_all(steps.reshape(n_rx * TP, 2, SLAB, feat // 2), ("rx", "tp"), 0, 0, tiled=True)
    def along(value, shift):
        return lax.ppermute(value, "ry", [(k, (k + shift) % n_ry) for k in range(n_ry)])

    def two_away(value):
        return lax.ppermute(value, "ry", [(k, (k + (2 if k % 2 else n_ry - 2)) % n_ry) for k in range(n_ry)])

    parts = call(
        functools.partial(first_body, n_rx), [shape((2, 2, SLAB, feat // 2))] * n_ry, [pos, group_x, terms], "ssv", name="first_round"
    )
    mids = [along(part, s) if s else part for s, part in zip(SHIFTS, parts)]

    def averaged(u, name):
        (news,) = call(
            functools.partial(second_body, u, n_ry), [shape((n_rx, 2, SLAB, feat // 2))], [pos, group_x, group_y, *mids],
            "sss" + "v" * n_ry, name="second_" + name,
        )
        news = lax.all_to_all(news, "rx", 0, 0, tiled=True)
        own, after, before, far = call(
            functools.partial(pick_body, n_rx, n_ry), [shape((n_rx, SLAB, feat // 2))] * 4, [pos, group_y, news], "ssv", name="pick_" + name
        )
        held = [own, two_away(far), along(after, 1), along(before, -1)]
        (out,) = call(functools.partial(last_body, n_rx), [shape((rows, width))], [pos, *held], "svvvv", name="last_" + name)
        return out

    new_down = averaged(0, "down")
    new_up = averaged(1, "up")
    return (in_grad[None, None], new_up[None, None], new_down[None, None])


def solution(mesh):
    in_specs = (
        P("rx", "ry", None, "tp"),
        P("rx", "ry", None, "tp"),
        P("rx", "ry", "tp", None),
        P("rx", "ry", "tp", None),
        P(),
        P(),
    )
    out_specs = (P("rx", "ry", None, "tp"), P("rx", "ry", "tp", None), P("rx", "ry", "tp", None))
    return jax.shard_map(shards, mesh=mesh, in_specs=in_specs, out_specs=out_specs, check_vma=False)
```
